32 devices in a mesh: dp: 4 (over y, x), fsdp: 8 (over z, core).
Axes of the slice: x: 2, y: 2, z: 4, core: 2. Of those that a mesh axis runs over, the one named last changes fastest.
Arguments:
- tokens: bfloat16 [25344, 768], P(('dp', 'fsdp')), may hold values from -6 to 6
- cotangent: bfloat16 [25344, 768], P(('dp', 'fsdp')), may hold values from -6 to 6
- keep_mask: int32 [128, 4], P(('dp', 'fsdp')), may hold values 0 or 1
- qkv_weight: float32 [2, 768, 2304], P(None, 'fsdp'), may hold values from -0.21875 to 0.21875
- proj_weight: float32 [2, 768, 768], P(None, 'fsdp'), may hold values from -1.25 to 1.25
- fc1_weight: float32 [2, 768, 3072], P(None, 'fsdp'), may hold values from -0.21875 to 0.21875
- fc2_weight: float32 [2, 3072, 768], P(None, 'fsdp'), may hold values from -0.109375 to 0.109375
- vectors: float32 [2, 9216], P(None, 'fsdp'), may hold values from -1.2 to 2.5, as said below
- qkv_first: float32 [2, 768, 2304], P(None, 'fsdp'), may hold values from -0.0004272461 to 0.0004272461
- qkv_second: float32 [2, 768, 2304], P(None, 'fsdp'), may hold values from 7.064254e-11 to 2.8257016e-10
- proj_first: float32 [2, 768, 768], P(None, 'fsdp'), may hold values from -0.0004272461 to 0.0004272461
- proj_second: float32 [2, 768, 768], P(None, 'fsdp'), may hold values from 7.064254e-11 to 2.8257016e-10
- fc1_first: float32 [2, 768, 3072], P(None, 'fsdp'), may hold values from -0.0004272461 to 0.0004272461
- fc1_second: float32 [2, 768, 3072], P(None, 'fsdp'), may hold values from 7.064254e-11 to 2.8257016e-10
- fc2_first: float32 [2, 3072, 768], P(None, 'fsdp'), may hold values from -0.0004272461 to 0.0004272461
- fc2_second: float32 [2, 3072, 768], P(None, 'fsdp'), may hold values from 7.064254e-11 to 2.8257016e-10
- vec_first: float32 [2, 9216], P(None, 'fsdp'), may hold values from -0.0012207031 to 0.0012207031
- vec_second: float32 [2, 9216], P(None, 'fsdp'), may hold values from 6.3578287e-10 to 2.5431315e-09
Outputs:
- output: bfloat16 [25344, 768], P(('dp', 'fsdp'))
- token_grad: float32 [25344, 768], P(('dp', 'fsdp'))
- grad_norm: float32 [], replicated
- qkv_grad: float32 [2, 768, 2304], P(None, 'fsdp')
- qkv_moment: float32 [2, 768, 2304], P(None, 'fsdp')
- qkv_new: float32 [2, 768, 2304], P(None, 'fsdp')
- proj_grad: float32 [2, 768, 768], P(None, 'fsdp')
- proj_moment: float32 [2, 768, 768], P(None, 'fsdp')
- proj_new: float32 [2, 768, 768], P(None, 'fsdp')
- fc1_grad: float32 [2, 768, 3072], P(None, 'fsdp')
- fc1_moment: float32 [2, 768, 3072], P(None, 'fsdp')
- fc1_new: float32 [2, 768, 3072], P(None, 'fsdp')
- fc2_grad: float32 [2, 3072, 768], P(None, 'fsdp')
- fc2_moment: float32 [2, 3072, 768], P(None, 'fsdp')
- fc2_new: float32 [2, 3072, 768], P(None, 'fsdp')
- vec_grad: float32 [2, 9216], P(None, 'fsdp')
- vec_moment: float32 [2, 9216], P(None, 'fsdp')
- vec_new: float32 [2, 9216], P(None, 'fsdp')
The draws below stay inside these ranges and needn't reach their ends.
Inputs may be any that keep to these rules, and one draw needn't show every extreme that they name: `keep_mask`: 1 keeps a residual branch of an image, 0 drops it. `vectors`: each row holds in order gain_one, shift_one, query_bias, value_bias, proj_bias, gain_two, shift_two, hidden_bias, out_bias; the gains are positive.
All inputs are finite; a program needn't handle non-finite values. No bound on the sum of `keep_mask` on one device may be relied on, other than what follows from the above.
Results may differ from the reference program's by a relative error of at most 0.022.
The reference program's roundings to bfloat16 on the way count: a program that leaves them out, or rounds other values in their place, can miss the bound.
Values may be sent and summed in bfloat16 or wider, within the bound.
A program may use at most 256 MiB of HBM per device.

```python
import math
import jax
import jax.numpy as jnp
from jax import lax

D = 768
HEADS = 12
HEAD_DIM = 64
FF = 3072
SEQ = 198
LAYERS = 2
STEP = 10
IMG_DEV = 4
VEC = 9216
IMAGES = 128
TOKENS = 25344
N_DP = 4


def rising_gain(key, low_end, high_end):
    position = jnp.arange(D, dtype=jnp.float32) / (D - 1)
    rough = jax.random.uniform(key, (LAYERS, D), jnp.float32, 0.85, 1.15)
    return (low_end + (high_end - low_end) * position)[None, :] * rough


def draw_vectors(key, part):
    key = jax.random.fold_in(key, 7)
    keys_list = jax.random.split(key, 4)
    gain_one = rising_gain(keys_list[0], 0.6, 1.8)
    gain_two = rising_gain(keys_list[1], 0.6, 1.8)
    shifts = jnp.clip(0.3 * jax.random.normal(keys_list[2], (LAYERS, 2 * D), jnp.float32), -1.2, 1.2)
    biases = jnp.clip(0.3 * jax.random.normal(keys_list[3], (LAYERS, 4 * D + FF), jnp.float32), -1.2, 1.2)
    return jnp.concatenate([gain_one, shifts[:, :D], biases[:, :3 * D], gain_two, shifts[:, D:], biases[:, 3 * D:]], axis=1)


def place_ends(drawn, stream_key, least, top_value):
    index_at = [jax.random.randint(jax.random.fold_in(stream_key, axis), (), 0, length) for axis, length in enumerate(drawn.shape)]
    longest = drawn.shape.index(max(drawn.shape))
    neighbour = index_at[:longest] + [(index_at[longest] + 1) % drawn.shape[longest]] + index_at[longest + 1:]
    return drawn.at[tuple(index_at)].set(least).at[tuple(neighbour)].set(top_value)


def level_of(rng, dims, cuts, least, top_value):
    def one(axis_at, blocks):
        heights = jax.random.uniform(jax.random.fold_in(jax.random.fold_in(rng, 6), axis_at), (blocks,), jnp.float32, least / len(cuts), top_value / len(cuts))
        return jnp.repeat(jnp.exp(heights), dims[axis_at] // blocks).reshape((-1,) + (1,) * (len(dims) - axis_at - 1))

    level = one(*cuts[0])
    for cut in cuts[1:]:
        level = level * one(*cut)
    return level


def normal_values(rng, dims, deviation, limit, cuts=(), kind=jnp.bfloat16):
    loudness = level_of(rng, dims, cuts, -0.22, 0.18) if cuts else 1.0
    values = jax.random.normal(rng, dims, jnp.float32) * deviation * loudness
    return jnp.minimum(jnp.maximum(values, -limit), limit).astype(kind)


def setup_inputs(seed: int = 0) -> dict:
    keys = jax.random.split(jax.random.key(seed), 19)
    return {
        "tokens": normal_values(keys[0], (TOKENS, D), 1.0, 6.0, ((0, 32),)),
        "cotangent": normal_values(keys[1], (TOKENS, D), 1.0, 6.0, ((0, 32),)),
        "keep_mask": place_ends((jax.random.randint(keys[2], (IMAGES, 2 * LAYERS), 0, 10) < 9).astype(jnp.int32), jax.random.fold_in(keys[2], 1), 0, 1),
        "qkv_weight": normal_values(keys[3], (LAYERS, D, 3 * D), D ** -0.5, 0.21875, ((1, 8),), jnp.float32),
        "proj_weight": normal_values(keys[4], (LAYERS, D, D), (D // 32) ** -0.5, 1.25, ((1, 8),), jnp.float32),
        "fc1_weight": normal_values(keys[5], (LAYERS, D, FF), D ** -0.5, 0.21875, ((1, 8),), jnp.float32),
        "fc2_weight": normal_values(keys[6], (LAYERS, FF, D), FF ** -0.5, 0.109375, ((1, 8),), jnp.float32),
        "vectors": draw_vectors(jax.random.fold_in(keys[18], 71), 0),
        "qkv_first": normal_values(keys[8], (LAYERS, D, 3 * D), (0.11 * (8 * D * D + 4 * D * FF) ** -0.5), 0.0004272461, ((1, 8),), jnp.float32),
        "qkv_second": jnp.clip(jnp.exp(math.log(2.825701617137355e-10) - 1.3862944 * jax.random.uniform(keys[9], (LAYERS, D, 3 * D), jnp.float32) ** level_of(keys[9], (LAYERS, D, 3 * D), ((1, 8),), -0.2, 0.2)), 7.064254042843388e-11, 2.825701617137355e-10),
        "proj_first": normal_values(keys[10], (LAYERS, D, D), (0.11 * (8 * D * D + 4 * D * FF) ** -0.5), 0.0004272461, ((1, 8),), jnp.float32),
        "proj_second": jnp.clip(jnp.exp(math.log(2.825701617137355e-10) - 1.3862944 * jax.random.uniform(keys[11], (LAYERS, D, D), jnp.float32) ** level_of(keys[11], (LAYERS, D, D), ((1, 8),), -0.2, 0.2)), 7.064254042843388e-11, 2.825701617137355e-10),
        "fc1_first": normal_values(keys[12], (LAYERS, D, FF), (0.11 * (8 * D * D + 4 * D * FF) ** -0.5), 0.0004272461, ((1, 8),), jnp.float32),
        "fc1_second": jnp.clip(jnp.exp(math.log(2.825701617137355e-10) - 1.3862944 * jax.random.uniform(keys[13], (LAYERS, D, FF), jnp.float32) ** level_of(keys[13], (LAYERS, D, FF), ((1, 8),), -0.2, 0.2)), 7.064254042843388e-11, 2.825701617137355e-10),
        "fc2_first": normal_values(keys[14], (LAYERS, FF, D), (0.11 * (8 * D * D + 4 * D * FF) ** -0.5), 0.0004272461, ((1, 8),), jnp.float32),
        "fc2_second": jnp.clip(jnp.exp(math.log(2.825701617137355e-10) - 1.3862944 * jax.random.uniform(keys[15], (LAYERS, FF, D), jnp.float32) ** level_of(keys[15], (LAYERS, FF, D), ((1, 8),), -0.2, 0.2)), 7.064254042843388e-11, 2.825701617137355e-10),
        "vec_first": normal_values(keys[16], (LAYERS, VEC), (0.33 * (8 * D * D + 4 * D * FF) ** -0.5), 0.0012207031, ((1, 8),), jnp.float32),
        "vec_second": jnp.clip(jnp.exp(math.log(2.543131483179195e-09) - 1.3862944 * jax.random.uniform(keys[17], (LAYERS, VEC), jnp.float32) ** level_of(keys[17], (LAYERS, VEC), ((1, 8),), -0.2, 0.2)), 6.357828707947988e-10, 2.543131483179195e-09),
    }


@jax.custom_vjp
def low(v):
    return lax.optimization_barrier(v.astype(jnp.bfloat16)).astype(jnp.float32)

@jax.custom_vjp
def low_back(v):
    return v

def low_keep(v):
    return (low(v), None)

def low_pass(kept, grad):
    return (grad,)

def back_keep(v):
    return (v, None)

def back_low(kept, grad):
    return (low(grad),)
low.defvjp(low_keep, low_pass)
low_back.defvjp(back_keep, back_low)
KEEP_RATE = 0.9
CLIP = 1.0
BETA_ONE = 0.9
BETA_TWO = 0.999
EPSILON = 1e-08
RATES = (0.08, 0.4, 0.08, 0.04, 0.5)
DECAYS = (0.05, 0.05, 0.05, 0.05, 0.0)
HIGH = lax.Precision.HIGHEST

def layer_norm(values, norm_gain, norm_shift):
    row_mean = lax.optimization_barrier(jnp.mean(values, -1, keepdims=True))
    centred = values - row_mean
    variance = lax.optimization_barrier(jnp.mean(centred * centred, -1, keepdims=True))
    return centred * lax.rsqrt(variance + 1e-06) * norm_gain + norm_shift

def gelu_exact(values):
    return jax.nn.gelu(values, approximate=False)

def split_vector(vector):
    return (vector[0:D], vector[D:2 * D], vector[2 * D:3 * D], vector[3 * D:4 * D], vector[4 * D:5 * D], vector[5 * D:6 * D], vector[6 * D:7 * D], vector[7 * D:7 * D + FF], vector[7 * D + FF:])

def block_apply(stream, params, keep_pair):
    w_qkv, w_proj, w_up, w_down, vector = params
    gain_one, shift_one, query_bias, value_bias, proj_bias, gain_two, shift_two, hidden_bias, out_bias = split_vector(vector)
    image_count = keep_pair.shape[0]
    normed = low(layer_norm(stream, gain_one, shift_one))
    qkv_bias = jnp.concatenate([query_bias, jnp.zeros_like(query_bias), value_bias])
    qkv_rows = low(low_back(jnp.dot(normed, w_qkv, precision=HIGH) + qkv_bias))
    query_rows = qkv_rows[:, :D].reshape(image_count, SEQ, HEADS, HEAD_DIM)
    key_rows = qkv_rows[:, D:2 * D].reshape(image_count, SEQ, HEADS, HEAD_DIM)
    value_rows = qkv_rows[:, 2 * D:].reshape(image_count, SEQ, HEADS, HEAD_DIM)
    raw_scores = jnp.einsum('nqhd,nkhd->nhqk', query_rows, key_rows, precision=HIGH)
    scores = low_back(raw_scores) * HEAD_DIM ** (-0.5)
    row_top = lax.optimization_barrier(jnp.max(scores, -1, keepdims=True))
    exp_scores = jnp.exp(scores - row_top)
    attn_probs = exp_scores / lax.optimization_barrier(jnp.sum(exp_scores, -1, keepdims=True))
    mixed_rows = jnp.einsum('nhqk,nkhd->nqhd', low(attn_probs), value_rows, precision=HIGH).reshape(image_count * SEQ, D)
    mixed_rows = low(low_back(mixed_rows))
    branch = low_back(jnp.dot(mixed_rows, w_proj, precision=HIGH) + proj_bias)
    middle = stream + branch * jnp.repeat(keep_pair[:, 0] / KEEP_RATE, SEQ)[:, None]
    normed_two = low(layer_norm(middle, gain_two, shift_two))
    hidden = low_back(jnp.dot(normed_two, w_up, precision=HIGH) + hidden_bias)
    active = low(gelu_exact(hidden))
    branch_two = low_back(jnp.dot(active, w_down, precision=HIGH) + out_bias)
    return middle + branch_two * jnp.repeat(keep_pair[:, 1] / KEEP_RATE, SEQ)[:, None]

def adamw_update(weight, gradient, first_old, second, factor, step_rate, weight_decay):
    clipped = gradient * factor
    new_first = BETA_ONE * first_old + (1.0 - BETA_ONE) * clipped
    new_second = BETA_TWO * second + (1.0 - BETA_TWO) * clipped * clipped
    first_hat = new_first / (1.0 - BETA_ONE ** STEP)
    second_hat = new_second / (1.0 - BETA_TWO ** STEP)
    new_weight = weight * (1.0 - step_rate * weight_decay) - step_rate * first_hat / (jnp.sqrt(second_hat) + EPSILON)
    return (clipped, new_second, new_weight)

def reference(tokens, cotangent, keep_mask, qkv_weight, proj_weight, fc1_weight, fc2_weight, vectors, qkv_first, qkv_second, proj_first, proj_second, fc1_first, fc1_second, fc2_first, fc2_second, vec_first, vec_second):
    keep_float = keep_mask.astype(jnp.float32)
    group_size = IMG_DEV * N_DP
    blocks = IMAGES // group_size

    def forward(stream, w_qkv, w_proj, w_up, w_down, vec_all):
        w_qkv = low(w_qkv)
        w_proj = low(w_proj)
        w_up = low(w_up)
        w_down = low(w_down)
        vec_all = low(vec_all)
        for which_layer in range(LAYERS):
            params = (w_qkv[which_layer], w_proj[which_layer], w_up[which_layer], w_down[which_layer], vec_all[which_layer])
            keep_pairs = keep_float[:, 2 * which_layer:2 * which_layer + 2].reshape(blocks, group_size, 2)

            def apply_group(block_pair, params=params):
                return block_apply(block_pair[0], params, block_pair[1])
            stream = lax.map(jax.checkpoint(apply_group), (stream.reshape(blocks, group_size * SEQ, D), keep_pairs)).reshape(IMAGES * SEQ, D)
        return stream
    result, pullback = jax.vjp(forward, tokens.astype(jnp.float32), qkv_weight, proj_weight, fc1_weight, fc2_weight, vectors)
    token_grad, grad_qkv, grad_proj, grad_up, grad_down, grad_vec = pullback(cotangent.astype(jnp.float32))
    grad_list = (grad_qkv, grad_proj, grad_up, grad_down, grad_vec)
    norm_square = jnp.sum(grad_qkv * grad_qkv) + jnp.sum(grad_proj * grad_proj) + jnp.sum(grad_up * grad_up)
    norm_square = norm_square + jnp.sum(grad_down * grad_down) + jnp.sum(grad_vec * grad_vec)
    grad_norm = jnp.sqrt(norm_square)
    factor = jnp.minimum(1.0, CLIP / (grad_norm + 1e-06))
    masters = (qkv_weight, proj_weight, fc1_weight, fc2_weight, vectors)
    firsts = (qkv_first, proj_first, fc1_first, fc2_first, vec_first)
    seconds = (qkv_second, proj_second, fc1_second, fc2_second, vec_second)
    updates = []
    for member in range(5):
        updates.extend(adamw_update(masters[member], grad_list[member], firsts[member], seconds[member], factor, RATES[member], DECAYS[member]))
    return (result.astype(jnp.bfloat16), token_grad, grad_norm, updates[0], updates[1], updates[2], updates[3], updates[4], updates[5], updates[6], updates[7], updates[8], updates[9], updates[10], updates[11], updates[12], updates[13], updates[14])
```

```python
import functools

import jax
import jax.numpy as jnp
from jax import lax
from jax.experimental import pallas as pl
from jax.experimental.pallas import tpu as pltpu
from jax.sharding import PartitionSpec as P

D = 768
HEADS = 12
HEAD_DIM = 64
FF = 3072
SEQ = 198
LAYERS = 2
STEP = 10


KEEP_RATE = 0.9
CLIP = 1.0
BETA_ONE = 0.9
BETA_TWO = 0.999
EPSILON = 1e-08
RATES = (0.08, 0.4, 0.08, 0.04, 0.5)
DECAYS = (0.05, 0.05, 0.05, 0.05, 0.0)


def layer_norm(values, norm_gain, norm_shift):
    row_mean = jnp.mean(values, -1, keepdims=True)
    centred = values - row_mean
    variance = jnp.mean(centred * centred, -1, keepdims=True)
    return centred * lax.rsqrt(variance + 1e-06) * norm_gain + norm_shift


def gelu_exact(values):
    return jax.nn.gelu(values, approximate=False)


def split_vector(vector):
    return (
        vector[0:D],
        vector[D : 2 * D],
        vector[2 * D : 3 * D],
        vector[3 * D : 4 * D],
        vector[4 * D : 5 * D],
        vector[5 * D : 6 * D],
        vector[6 * D : 7 * D],
        vector[7 * D : 7 * D + FF],
        vector[7 * D + FF :],
    )


def scaled(values, factors):
    image_count = factors.shape[0]
    return (values.reshape(image_count, -1, values.shape[-1]) * factors[:, None, None]).reshape(
        values.shape
    )


def block_forward(stream, params, keep_pair):
    w_qkv, w_proj, w_up, w_down, vec_low = params
    (
        gain_one,
        shift_one,
        query_bias,
        value_bias,
        proj_bias,
        gain_two,
        shift_two,
        hidden_bias,
        out_bias,
    ) = split_vector(vec_low.astype(jnp.float32))
    image_count = keep_pair.shape[0]
    normed = layer_norm(stream, gain_one, shift_one).astype(jnp.bfloat16)
    qkv_bias = jnp.concatenate([query_bias, jnp.zeros_like(query_bias), value_bias])
    qkv_rows = (jnp.dot(normed, w_qkv, preferred_element_type=jnp.float32) + qkv_bias).astype(
        jnp.bfloat16
    )
    query_rows = qkv_rows[:, :D].reshape(image_count, SEQ, HEADS, HEAD_DIM)
    key_rows = qkv_rows[:, D : 2 * D].reshape(image_count, SEQ, HEADS, HEAD_DIM)
    value_rows = qkv_rows[:, 2 * D :].reshape(image_count, SEQ, HEADS, HEAD_DIM)
    raw_scores = jnp.einsum(
        "nqhd,nkhd->nhqk", query_rows, key_rows, preferred_element_type=jnp.float32
    )
    scores = raw_scores * HEAD_DIM ** (-0.5)
    row_top = jnp.max(scores, -1, keepdims=True)
    exp_scores = jnp.exp(scores - row_top)
    attn_probs = exp_scores / jnp.sum(exp_scores, -1, keepdims=True)
    attn_low = attn_probs.astype(jnp.bfloat16)
    mixed_rows = jnp.einsum(
        "nhqk,nkhd->nqhd", attn_low, value_rows, preferred_element_type=jnp.float32
    )
    mixed_rows = mixed_rows.reshape(image_count * SEQ, D).astype(jnp.bfloat16)
    branch = jnp.dot(mixed_rows, w_proj, preferred_element_type=jnp.float32) + proj_bias
    middle = stream + scaled(branch, keep_pair[:, 0] / KEEP_RATE)
    normed_two = layer_norm(middle, gain_two, shift_two).astype(jnp.bfloat16)
    hidden = jnp.dot(normed_two, w_up, preferred_element_type=jnp.float32) + hidden_bias
    active = gelu_exact(hidden).astype(jnp.bfloat16)
    branch_two = jnp.dot(active, w_down, preferred_element_type=jnp.float32) + out_bias
    result = middle + scaled(branch_two, keep_pair[:, 1] / KEEP_RATE)
    saved = (
        normed,
        query_rows,
        key_rows,
        value_rows,
        attn_probs,
        attn_low,
        mixed_rows,
        middle,
        normed_two,
        hidden,
        active,
    )
    return (result, saved)


def block_backward(stream, params, keep_pair, grad_out):
    w_qkv, w_proj, w_up, w_down, vec_low = params
    (
        gain_one,
        shift_one,
        query_bias,
        value_bias,
        proj_bias,
        gain_two,
        shift_two,
        hidden_bias,
        out_bias,
    ) = split_vector(vec_low.astype(jnp.float32))
    unused, saved = block_forward(stream, params, keep_pair)
    (
        normed,
        query_rows,
        key_rows,
        value_rows,
        attn_probs,
        attn_low,
        mixed_rows,
        middle,
        normed_two,
        hidden,
        active,
    ) = saved
    image_count = keep_pair.shape[0]
    row_count = stream.shape[0]
    d_branch_two = scaled(grad_out, keep_pair[:, 1] / KEEP_RATE).astype(jnp.bfloat16)
    grad_down = jnp.einsum("rf,rd->fd", active, d_branch_two, preferred_element_type=jnp.float32)
    grad_out_bias = jnp.sum(d_branch_two.astype(jnp.float32), 0)
    d_active = jnp.einsum("rd,fd->rf", d_branch_two, w_down, preferred_element_type=jnp.float32)
    unused_two, gelu_back = jax.vjp(gelu_exact, hidden)
    d_hidden = gelu_back(d_active)[0].astype(jnp.bfloat16)
    grad_up = jnp.einsum("rd,rf->df", normed_two, d_hidden, preferred_element_type=jnp.float32)
    grad_hidden_bias = jnp.sum(d_hidden.astype(jnp.float32), 0)
    d_normed_two = jnp.einsum("rf,df->rd", d_hidden, w_up, preferred_element_type=jnp.float32)
    unused_three, norm_back_two = jax.vjp(layer_norm, middle, gain_two, shift_two)
    d_middle_part, grad_gain_two, grad_shift_two = norm_back_two(d_normed_two)
    d_middle = grad_out + d_middle_part
    d_branch = scaled(d_middle, keep_pair[:, 0] / KEEP_RATE).astype(jnp.bfloat16)
    grad_proj = jnp.einsum("rd,re->de", mixed_rows, d_branch, preferred_element_type=jnp.float32)
    grad_proj_bias = jnp.sum(d_branch.astype(jnp.float32), 0)
    d_mixed = jnp.einsum("re,de->rd", d_branch, w_proj, preferred_element_type=jnp.float32).astype(
        jnp.bfloat16
    )
    d_mixed = d_mixed.reshape(image_count, SEQ, HEADS, HEAD_DIM)
    d_probs = jnp.einsum("nqhd,nkhd->nhqk", d_mixed, value_rows, preferred_element_type=jnp.float32)
    grad_value = jnp.einsum(
        "nhqk,nqhd->nkhd", attn_low, d_mixed, preferred_element_type=jnp.float32
    )
    row_delta = jnp.sum(attn_probs * d_probs, -1, keepdims=True)
    d_raw = (attn_probs * (d_probs - row_delta) * HEAD_DIM ** (-0.5)).astype(jnp.bfloat16)
    grad_query = jnp.einsum("nhqk,nkhd->nqhd", d_raw, key_rows, preferred_element_type=jnp.float32)
    grad_key = jnp.einsum("nhqk,nqhd->nkhd", d_raw, query_rows, preferred_element_type=jnp.float32)
    d_qkv = jnp.concatenate(
        [
            grad_query.reshape(row_count, D),
            grad_key.reshape(row_count, D),
            grad_value.reshape(row_count, D),
        ],
        axis=1,
    ).astype(jnp.bfloat16)
    grad_qkv = jnp.einsum("rd,re->de", normed, d_qkv, preferred_element_type=jnp.float32)
    grad_query_bias = jnp.sum(d_qkv[:, :D].astype(jnp.float32), 0)
    grad_value_bias = jnp.sum(d_qkv[:, 2 * D :].astype(jnp.float32), 0)
    d_normed = jnp.einsum("re,de->rd", d_qkv, w_qkv, preferred_element_type=jnp.float32)
    unused_four, norm_back_one = jax.vjp(layer_norm, stream, gain_one, shift_one)
    d_stream_part, grad_gain_one, grad_shift_one = norm_back_one(d_normed)
    grad_in = d_middle + d_stream_part
    grad_vector = jnp.concatenate(
        [
            grad_gain_one,
            grad_shift_one,
            grad_query_bias,
            grad_value_bias,
            grad_proj_bias,
            grad_gain_two,
            grad_shift_two,
            grad_hidden_bias,
            grad_out_bias,
        ]
    )
    return (grad_in, (grad_qkv, grad_proj, grad_up, grad_down, grad_vector))


def adamw_update(weight, gradient, first_old, second, factor, step_rate, weight_decay):
    clipped = gradient * factor
    new_first = BETA_ONE * first_old + (1.0 - BETA_ONE) * clipped
    new_second = BETA_TWO * second + (1.0 - BETA_TWO) * clipped * clipped
    first_hat = new_first / (1.0 - BETA_ONE**STEP)
    second_hat = new_second / (1.0 - BETA_TWO**STEP)
    new_weight = weight * (1.0 - step_rate * weight_decay) - step_rate * first_hat / (
        jnp.sqrt(second_hat) + EPSILON
    )
    return (clipped, new_second, new_weight)


MESH_ID = pl.DeviceIdType.MESH
ROWS = 96
LOW = jnp.bfloat16
MIB = 1 << 20


def place():
    dp, fs = lax.axis_index("dp"), lax.axis_index("fsdp")
    return dp, fs, lax.div(dp, 2), lax.rem(dp, 2), lax.div(fs, 2), lax.rem(fs, 2)


def greet(peers):
    barrier = pltpu.get_barrier_semaphore()
    for peer in peers:
        pl.semaphore_signal(barrier, inc=1, device_id=peer, device_id_type=MESH_ID)
    pl.semaphore_wait(barrier, len(peers))


def sender(send, recv):
    started = {}

    def start(key, at, src, dst, device):
        copy = pltpu.make_async_remote_copy(
            src_ref=src,
            dst_ref=dst,
            send_sem=send.at[at],
            recv_sem=recv.at[at],
            device_id=device,
            device_id_type=MESH_ID,
        )
        copy.start()
        started[key] = copy

    return started, start


HOP = 1.5


class Course:
    def __init__(self):
        self.now = 0.0
        self.free = {}
        self.lines = {}

    def add(self, name, steps, delay=0.0):
        self.lines[name] = [0, self.now + delay, steps]

    def take(self, name):
        line = self.lines[name]
        step, link, cost = line[2][line[0]]
        line[0] += 1
        self.now = max(self.now, line[1])
        step()
        end = max(self.now, self.free.get(link, 0.0)) + cost
        self.free[link] = end
        line[1] = end + HOP

    def earliest(self):
        waiting = [
            (line[1], name) for name, line in self.lines.items() if line[0] < len(line[2])
        ]
        return min(waiting, key=lambda item: item[0]) if waiting else None

    def spend(self, cost):
        self.now += cost
        while True:
            following = self.earliest()
            if following is None or following[0] > self.now:
                return
            self.take(following[1])

    def require(self, name, count):
        while self.lines[name][0] < count:
            following = self.earliest()
            if following[0] >= self.lines[name][1]:
                following = (0.0, name)
            self.take(following[1])

    def drain(self):
        while (following := self.earliest()) is not None:
            self.take(following[1])


def gather_lines(
    course, round_shard, landed, vec, full_ab, full_c, vec_full, send, recv, vec_send, vec_recv, vec_own
):
    dp, fs, y, x, z, c = place()
    q_x, q_y, q_d = y * 2 + 1 - x, (1 - y) * 2 + x, (1 - y) * 2 + 1 - x
    to_x, to_y, to_core = (q_x, fs), (q_y, fs), (dp, z * 2 + 1 - c)
    inner = jnp.logical_or(z == 1, z == 2)
    pair, far, farthest = z + 1 - 2 * lax.rem(z, 2), 2 - lax.div(z, 2), 3 - 3 * lax.div(z, 2)
    behind = [pair, far, farthest]
    to_pair, to_middle = (dp, pair * 2 + c), (dp, (3 - z) * 2 + c)
    others = [(dp, lax.rem(fs + k, 8)) for k in range(1, 8)]
    started, start = sender(send, recv)
    vec_started, vec_start = sender(vec_send, vec_recv)

    def slot(i, q, zz, cc):
        layer, group = divmod(i, 3)
        return full_c.at[layer, zz, cc, q] if group == 2 else full_ab.at[layer, group, q, zz, cc]

    def column(i, q, cc):
        layer, group = divmod(i, 3)
        return full_c.at[layer, :, cc, q] if group == 2 else full_ab.at[layer, group, q, :, cc]

    def z_copy(i, kind):
        piece = slot(i, dp, (z, z, pair, far, farthest)[kind], c)
        return pltpu.make_async_remote_copy(
            src_ref=piece,
            dst_ref=piece,
            send_sem=send.at[i, (0, 1, 2, 19, 20)[kind]],
            recv_sem=recv.at[i, (0, 1, 2, 1, 2)[kind]],
            device_id=(to_pair, to_middle, to_middle, to_pair, to_pair)[kind],
            device_id_type=MESH_ID,
        )

    def along_z(i):
        round_shard(i)
        z_copy(i, 0).start()

        @pl.when(inner)
        def _():
            z_copy(i, 1).start()

    def one_side(i, k):
        piece = slot(i, dp, behind[k], c)
        start((i, 3 + k), (i, 3 + k), piece, piece, to_x)
        start((i, 6 + k), (i, 6 + k), piece, piece, to_y)

    def pass_on(i):
        z_copy(i, 0).wait_recv()

        @pl.when(inner)
        def _():
            z_copy(i, 2).start()

        one_side(i, 0)

    def pass_back(i):
        @pl.when(inner)
        def _():
            z_copy(i, 1).wait_recv()
            z_copy(i, 3).start()
            z_copy(i, 2).wait_recv()
            z_copy(i, 4).start()

    def to_sides(i):
        @pl.when(jnp.logical_not(inner))
        def _():
            z_copy(i, 1).wait_recv()
            z_copy(i, 2).wait_recv()

        one_side(i, 1)
        one_side(i, 2)
        start((i, 15), (i, 15), column(i, dp, c), column(i, dp, c), to_core)

    def to_corner(i):
        for k in range(3):
            started[i, 3 + k].wait_recv()
            piece = slot(i, q_x, behind[k], c).at[pl.ds(0, ROWS // 2)]
            start((i, 9 + k), (i, 9 + k), piece, piece, to_y)
            started[i, 6 + k].wait_recv()
            piece = slot(i, q_y, behind[k], c).at[pl.ds(ROWS // 2, ROWS // 2)]
            start((i, 12 + k), (i, 12 + k), piece, piece, to_x)
        for j, q in ((16, q_x), (17, q_y)):
            start((i, j), (i, j), column(i, q, c), column(i, q, c), to_core)

    def to_sibling(i):
        for k in range(3):
            started[i, 9 + k].wait_recv()
            started[i, 12 + k].wait_recv()
        start((i, 18), (i, 18), column(i, q_d, c), column(i, q_d, c), to_core)

    def finish(i):
        for j in range(15, 19):
            started[i, j].wait_recv()
        landed(i)

    def vec_ready():
        vec_copy.wait()
        for k in range(7):
            vec_started[k].wait_recv()

    def close():
        for copy in started.values():
            copy.wait_send()
        for i in range(3 * LAYERS):
            z_copy(i, 0).wait_send()

        @pl.when(inner)
        def _():
            for i in range(3 * LAYERS):
                for kind in range(1, 5):
                    z_copy(i, kind).wait_send()

        for copy in vec_started.values():
            copy.wait_send()

    greet([to_x, to_y] + others)
    vec_copy = pltpu.make_async_copy(vec, vec_full.at[fs], vec_own.at[0])
    vec_copy.start()
    for k in range(7):
        vec_start(k, k, vec, vec_full.at[fs], others[k])
    count = 3 * LAYERS
    course.add("vec", [(vec_ready, "none", 0.0)], 4.0)
    for i in range(count):
        course.add(
            i,
            [
                (functools.partial(along_z, i), "z", 3.2),
                (functools.partial(pass_on, i), "middle", 3.2),
                (functools.partial(pass_back, i), "z", 6.4),
                (functools.partial(to_sides, i), "xy", 9.0),
                (functools.partial(to_corner, i), "xy", 4.7),
                (functools.partial(to_sibling, i), "core", 1.5),
                (functools.partial(finish, i), "none", 0.0),
            ],
            13.7 * i,
        )
    return close


IMG_DEV = 4
PAD = 208
PADDED = IMG_DEV * PAD
PAIRS = HEADS // 2
WIDE = 2 * HEAD_DIM
TILE = 256
STEP_ROWS = 16
WIDTH = 12 * D
GAIN_ONE, SHIFT_ONE, QUERY_BIAS, VALUE_BIAS, PROJ_BIAS, GAIN_TWO, SHIFT_TWO, HIDDEN_BIAS = (
    at * D for at in range(8)
)
OUT_BIAS = HIDDEN_BIAS + FF
F32 = jnp.float32


def nn(left, right):
    return lax.dot_general(left, right, (((1,), (0,)), ((), ())), preferred_element_type=F32)


def nt(left, right):
    return lax.dot_general(left, right, (((1,), (1,)), ((), ())), preferred_element_type=F32)


def tn(left, right):
    return lax.dot_general(left, right, (((0,), (0,)), ((), ())), preferred_element_type=F32)


def tile_of(step, size):
    return pl.ds(pl.multiple_of(step * size, size), size)


def over(count, body, unroll=1):
    def step(at, carry):
        body(at)
        return carry

    lax.fori_loop(0, count, step, 0, unroll=unroll)


def kept(mask, image, column):
    return mask[image, column].astype(F32) * (1.0 / KEEP_RATE)


def row_norm(stream, held, scale, normed, row, gain_at, shift_at):
    gain, shift = row[0:1, gain_at : gain_at + D], row[0:1, shift_at : shift_at + D]

    def body(step):
        rows = tile_of(step, STEP_ROWS)
        values = stream[rows]
        centred = values - jnp.mean(values, -1, keepdims=True)
        inverse = lax.rsqrt(jnp.mean(centred * centred, -1, keepdims=True) + 1e-06)
        unit = centred * inverse
        held[rows] = unit.astype(LOW)
        scale[rows] = jnp.broadcast_to(inverse, (STEP_ROWS, 128))
        normed[rows] = (unit * gain + shift).astype(LOW)

    over(PADDED // STEP_ROWS, body, 13)


def project_qkv(normed, weight, row, qkv):
    for block, bias_at in enumerate((QUERY_BIAS, None, VALUE_BIAS)):

        def body(step, block=block, bias_at=bias_at):
            columns = tile_of(step, TILE)
            values = nn(normed[...], weight[block, :, columns])
            if bias_at is not None:
                values = values + row[0:1, pl.ds(pl.multiple_of(bias_at + step * TILE, TILE), TILE)]
            qkv[:, pl.ds(pl.multiple_of(block * D + step * TILE, TILE), TILE)] = values.astype(LOW)

        over(D // TILE, body, D // TILE)


def identity(size):
    row = lax.broadcasted_iota(jnp.int32, (size, size), 0)
    lane = lax.broadcasted_iota(jnp.int32, (size, size), 1)
    return (row == lane).astype(F32).astype(LOW)


def head_lanes(halves):
    lane = lax.broadcasted_iota(jnp.int32, (PAD, WIDE), 1)
    halves[0] = (lane < HEAD_DIM).astype(F32).astype(LOW)
    halves[1] = (lane >= HEAD_DIM).astype(F32).astype(LOW)


def real_keys(raw):
    key = lax.broadcasted_iota(jnp.int32, (STEP_ROWS, PAD), 0) + (PAD - STEP_ROWS)
    last = jnp.where(key < SEQ, raw[PAD - STEP_ROWS :], -1e30)
    return jnp.concatenate([raw[: PAD - STEP_ROWS], last], axis=0)


SHARP = HEAD_DIM ** (-0.5) * 1.4426950408889634


def attend(qkv, mixed, level, eye, halves, image):
    def one(step, at):
        pair, rows = step * 3 + at, pl.ds(image * PAD, PAD)
        query = qkv[rows, pl.ds(pl.multiple_of(pair * WIDE, WIDE), WIDE)]
        key = qkv[rows, pl.ds(pl.multiple_of(D + pair * WIDE, WIDE), WIDE)]
        value = qkv[rows, pl.ds(pl.multiple_of(2 * D + pair * WIDE, WIDE), WIDE)]
        turned = value.T
        scores = nt(jnp.concatenate([key * halves[0], key * halves[1]], axis=0), query)
        sides = []
        for head in range(2):
            raw = real_keys(scores[head * PAD : (head + 1) * PAD])
            top = jnp.max(raw, 0, keepdims=True)
            weights = jnp.exp2((raw - top) * SHARP)
            total = jnp.sum(weights, 0, keepdims=True)
            level[image, 2 * pair + head] = top * SHARP + jnp.log(total) * 1.4426950408889634
            low = (weights * (1.0 / total)).astype(LOW)
            sides.append(nn(turned[head * HEAD_DIM : (head + 1) * HEAD_DIM], low))
        both = jnp.concatenate(sides, axis=0).astype(LOW)
        mixed[rows, pl.ds(pl.multiple_of(pair * WIDE, WIDE), WIDE)] = both.T

    def body(step):
        for at in range(3):
            one(step, at)

    over(2, body)


def add_branch(stream, values, weights, row, bias_at, drop, drop_at):
    def body(step):
        columns = tile_of(step, TILE)
        branch = nn(values[...], weights[:, columns])
        branch = branch + row[0:1, pl.ds(pl.multiple_of(bias_at + step * TILE, TILE), TILE)]
        for image in range(IMG_DEV):
            rows = pl.ds(image * PAD, PAD)
            stream[rows, columns] = (
                stream[rows, columns]
                + branch[image * PAD : (image + 1) * PAD] * kept(drop, image, drop_at)
            )

    over(D // TILE, body, D // TILE)


def normal_parts(values):
    bell = jnp.exp2((values * values) * (-0.5 * 1.4426950408889634))
    size = 1.0 + (0.3275911 * 0.5**0.5) * jnp.abs(values)
    part = pl.reciprocal(size, approx=True)
    part = part * (2.0 - size * part)
    tail = 0.5 * 1.061405429 * part - 0.5 * 1.453152027
    for factor in (1.421413741, -0.284496736, 0.254829592):
        tail = tail * part + 0.5 * factor
    tail = tail * part * bell
    return jnp.where(values >= 0.0, 1.0 - tail, tail), bell


def hidden_units(normed, weight, row, active, slope, first):
    def body(step):
        tile = first + step
        block, within = lax.div(tile, 3), lax.rem(tile, 3)
        at = pl.multiple_of(tile * TILE, TILE)
        hidden = nn(normed[...], weight[block, :, tile_of(within, TILE)])
        bias = row[0:1, pl.ds(pl.multiple_of(HIDDEN_BIAS + at, TILE), TILE)]
        for part in range(PADDED // STEP_ROWS):
            rows = slice(part * STEP_ROWS, (part + 1) * STEP_ROWS)
            values = hidden[rows] + bias
            chance, bell = normal_parts(values)
            active[rows, pl.ds(at, TILE)] = (values * chance).astype(LOW)
            slope[rows, pl.ds(at, TILE)] = (
                chance + values * bell * (2.0 * jnp.pi) ** (-0.5)
            ).astype(LOW)

    over(4, body, 2)


SAVED = (
    ("unit_one", (PADDED, D), LOW),
    ("scale_one", (PADDED, 128), F32),
    ("normed_one", (PADDED, D), LOW),
    ("qkv", (PADDED, 3 * D), LOW),
    ("level", (IMG_DEV, HEADS, 1, PAD), F32),
    ("mixed", (PADDED, D), LOW),
    ("unit_two", (PADDED, D), LOW),
    ("scale_two", (PADDED, 128), F32),
    ("normed_two", (PADDED, D), LOW),
    ("active", (PADDED, FF), LOW),
    ("slope", (PADDED, FF), LOW),
)


def vec_row(vec_full, layer, row):
    for shard in range(8):
        for part in range(9):
            at = (shard * 9 + part) * 128
            row[0:1, at : at + 128] = vec_full[shard, layer, part].astype(LOW).astype(F32)


def pad_image(padded, rows, image):
    padded[image * PAD : image * PAD + SEQ] = rows[image * SEQ : (image + 1) * SEQ].astype(F32)
    padded[image * PAD + SEQ : (image + 1) * PAD] = jnp.zeros((PAD - SEQ, D), F32)


def forward_kernel(
    tokens, drop, vec, *rest
):
    masters, (out_ab, out_c, vec_rows, output), rest = rest[:4], rest[4:8], rest[8:]
    names = [name for name, _, _ in SAVED]
    saved = dict(zip(names, rest[: len(SAVED)]))
    held = dict(zip(names, rest[len(SAVED) : 2 * len(SAVED)]))
    (
        stream, vec_full, eye, halves, wide, vec_mine, full_ab, full_c, send, recv, vec_send, vec_recv,
        vec_own, weight_sem, save_sem, wide_sem,
    ) = rest[2 * len(SAVED) :]
    dp, fs, y, x, z, c = place()
    course = Course()
    fetched, pending, kept_weights = {}, {}, []

    def fetch(i):
        layer, group = divmod(i, 3)
        if group == 0:
            pairs = [(masters[0].at[layer, :, pl.ds(q * D, D)], q) for q in range(3)]
            pairs.append((masters[1].at[layer], 3))
        elif group == 1:
            pairs = [(masters[2].at[layer, :, pl.ds(q * D, D)], q) for q in range(4)]
        else:
            pairs = [(masters[3].at[layer, pl.ds(q * ROWS, ROWS)], q) for q in range(4)]
        fetched[i] = []
        for source, q in pairs:
            copy = pltpu.make_async_copy(source, wide.at[i % 2, q], wide_sem.at[i % 2, q])
            copy.start()
            fetched[i].append(copy)

    def round_shard(i):
        layer, group = divmod(i, 3)
        for copy in fetched[i]:
            copy.wait()

        def body(step):
            q, rows = lax.div(step, ROWS // STEP_ROWS), tile_of(lax.rem(step, ROWS // STEP_ROWS), STEP_ROWS)
            values = wide[i % 2, q, rows].astype(LOW)
            if group == 2:
                full_c[layer, z, c, q, rows] = values
            else:
                full_ab[layer, group, q, z, c, rows] = values

        over(4 * ROWS // STEP_ROWS, body, 4)
        if i + 2 < 3 * LAYERS:
            fetch(i + 2)

    def landed(i):
        layer, group = divmod(i, 3)
        if group == 2:
            source, target = full_c.at[layer], out_c.at[layer]
        else:
            source, target = full_ab.at[layer, group], out_ab.at[layer, group]
        copy = pltpu.make_async_copy(source, target, weight_sem.at[i])
        copy.start()
        kept_weights.append(copy)

    def weight_of(i):
        course.require(i, 7)
        layer, group = divmod(i, 3)
        if group == 2:
            return full_c.at[layer].reshape(FF, D)
        return full_ab.at[layer, group].reshape(4, D, D)

    fetch(0)
    fetch(1)
    for layer in range(LAYERS):
        for part in range(9):
            vec_mine[layer, part] = vec[layer : layer + 1, part * 128 : (part + 1) * 128]
    close = gather_lines(
        course, round_shard, landed, vec_mine, full_ab, full_c, vec_full, send, recv, vec_send, vec_recv, vec_own
    )

    def save(layer, name):
        at = names.index(name)
        copy = pltpu.make_async_copy(held[name], saved[name].at[layer], save_sem.at[at])
        copy.start()
        pending[name] = copy

    def free(*which):
        for name in which:
            if name in pending:
                pending.pop(name).wait()

    course.spend(0.0)
    eye[...] = identity(TILE)
    head_lanes(halves)
    for image in range(IMG_DEV):
        pad_image(stream, tokens, image)
    course.spend(1.0)
    course.require("vec", 1)
    for layer in range(LAYERS):
        row = vec_rows.at[pl.ds(layer, 1)]
        vec_row(vec_full, layer, row)
        free("unit_one", "scale_one", "normed_one")
        row_norm(stream, held["unit_one"], held["scale_one"], held["normed_one"], row, GAIN_ONE, SHIFT_ONE)
        for name in ("unit_one", "scale_one", "normed_one"):
            save(layer, name)
        course.spend(3.0)
        weight = weight_of(3 * layer)
        free("qkv")
        project_qkv(held["normed_one"], weight, row, held["qkv"])
        save(layer, "qkv")
        course.spend(5.0)
        free("level", "mixed")
        for image in range(IMG_DEV):
            attend(held["qkv"], held["mixed"], held["level"], eye, halves, image)
            course.spend(3.0)
        save(layer, "level")
        save(layer, "mixed")
        add_branch(stream, held["mixed"], weight.at[3], row, PROJ_BIAS, drop, 2 * layer)
        course.spend(2.0)
        free("unit_two", "scale_two", "normed_two")
        row_norm(stream, held["unit_two"], held["scale_two"], held["normed_two"], row, GAIN_TWO, SHIFT_TWO)
        for name in ("unit_two", "scale_two", "normed_two"):
            save(layer, name)
        course.spend(3.0)
        weight = weight_of(3 * layer + 1)
        free("active", "slope")
        for first in (0, 4, 8):
            hidden_units(held["normed_two"], weight, row, held["active"], held["slope"], first)
            course.spend(5.0)
        save(layer, "active")
        save(layer, "slope")
        weight = weight_of(3 * layer + 2)
        add_branch(stream, held["active"], weight, row, OUT_BIAS, drop, 2 * layer + 1)
        course.spend(6.0)

    def narrow(step):
        rows = tile_of(step, STEP_ROWS)
        output[rows] = stream[rows].astype(LOW)

    over(PADDED // STEP_ROWS, narrow, 4)
    course.drain()
    close()
    free(*names)
    for copy in kept_weights:
        copy.wait()


def forward_call(tokens, drop, vec, masters):
    count = 3 * LAYERS
    dma = pltpu.SemaphoreType.DMA
    any_space = pl.BlockSpec(memory_space=pl.ANY)
    vmem = pl.BlockSpec(memory_space=pltpu.VMEM)
    outs = pl.pallas_call(
        forward_kernel,
        out_shape=[
            jax.ShapeDtypeStruct((LAYERS, 2, 4, 4, 2, ROWS, D), LOW),
            jax.ShapeDtypeStruct((LAYERS, 4, 2, 4, ROWS, D), LOW),
            jax.ShapeDtypeStruct((LAYERS, WIDTH), F32),
            jax.ShapeDtypeStruct((PADDED, D), LOW),
        ]
        + [jax.ShapeDtypeStruct((LAYERS,) + shape, kind) for _, shape, kind in SAVED],
        in_specs=[vmem, pl.BlockSpec(memory_space=pltpu.SMEM), vmem] + [any_space] * 4,
        out_specs=[any_space, any_space, vmem, vmem] + [any_space] * len(SAVED),
        scratch_shapes=[pltpu.VMEM(shape, kind) for _, shape, kind in SAVED]
        + [
            pltpu.VMEM((PADDED, D), F32),
            pltpu.VMEM((8, LAYERS, 9, 1, 128), F32),
            pltpu.VMEM((TILE, TILE), LOW),
            pltpu.VMEM((2, PAD, WIDE), LOW),
            pltpu.VMEM((2, 4, ROWS, D), F32),
            pltpu.VMEM((LAYERS, 9, 1, 128), F32),
            pltpu.VMEM((LAYERS, 2, 4, 4, 2, ROWS, D), LOW),
            pltpu.VMEM((LAYERS, 4, 2, 4, ROWS, D), LOW),
            dma((count, 21)),
            dma((count, 21)),
            dma((7,)),
            dma((7,)),
            dma((1,)),
            dma((count,)),
            dma((len(SAVED),)),
            dma((2, 4)),
        ],
        compiler_params=pltpu.CompilerParams(
            collective_id=0, has_side_effects=True, vmem_limit_bytes=63 * MIB
        ),
        name="forward_and_gather",
    )(tokens, drop, vec, *masters)
    return outs[:4], dict(zip([name for name, _, _ in SAVED], outs[4:]))


def fold(values):
    return values[0:8] + values[8:16]


def nothing(count=1):
    return tuple(jnp.zeros((8, D), F32) for _ in range(count))


def column(total):
    return jnp.sum(total, 0, keepdims=True)


def scale_rows(gradient, low, drop, drop_at):
    def body(step, total):
        rows = tile_of(step, STEP_ROWS)
        factor = kept(drop, lax.div(step, PAD // STEP_ROWS), drop_at)
        values = (gradient[rows] * factor).astype(LOW)
        low[rows] = values
        return total + fold(values.astype(F32))

    return column(lax.fori_loop(0, PADDED // STEP_ROWS, body, nothing()[0], unroll=13))


def norm_back(part, unit, scale, gradient, gain, low=None, drop=None, drop_at=None):
    def body(step, totals):
        rows = tile_of(step, STEP_ROWS)
        values, units = part[rows], unit[rows].astype(F32)
        scaled_values = values * gain
        first = jnp.mean(scaled_values, -1, keepdims=True)
        second = jnp.mean(scaled_values * units, -1, keepdims=True)
        new = gradient[rows] + scale[rows][:, 0:1] * (scaled_values - first - units * second)
        gradient[rows] = new
        sums = [fold(values * units), fold(values)]
        if low is not None:
            factor = kept(drop, lax.div(step, PAD // STEP_ROWS), drop_at)
            rounded = (new * factor).astype(LOW)
            low[rows] = rounded
            sums.append(fold(rounded.astype(F32)))
        return tuple(total + item for total, item in zip(totals, sums))

    count = 2 if low is None else 3
    totals = lax.fori_loop(0, PADDED // STEP_ROWS, body, nothing(count), unroll=13)
    return [column(total) for total in totals]


def hidden_back(low, weight, slope, vec_grad, first):
    def body(step):
        tile = first + step
        block, within = lax.div(tile, 3), lax.rem(tile, 3)
        at = pl.multiple_of(tile * TILE, TILE)
        values = nt(low[...], weight[tile_of(within, TILE), tile_of(block, D)])
        values = (values * slope[:, pl.ds(at, TILE)].astype(F32)).astype(LOW)
        slope[:, pl.ds(at, TILE)] = values
        vec_grad[0:1, pl.ds(pl.multiple_of(HIDDEN_BIAS + at, TILE), TILE)] = jnp.sum(
            values.astype(F32), 0, keepdims=True
        )

    over(6, body, 3)


def spread_back(rows_low, weight, width, part):
    def body(step):
        tile = tile_of(step, TILE)
        part[:, tile] = nt(rows_low[:, 0:width], weight[tile, 0:width])

    over(D // TILE, body, D // TILE)


def attend_back(qkv, level, d_mixed, d_qkv, eye, halves, image):
    def one(step, at):
        pair, rows = step * 3 + at, pl.ds(image * PAD, PAD)
        columns = [
            pl.ds(pl.multiple_of(third * D + pair * WIDE, WIDE), WIDE) for third in range(3)
        ]
        query, key, value = (qkv[rows, part] for part in columns)
        d_rows = d_mixed[rows, columns[0]]
        small_key, small_query = key * HEAD_DIM ** (-0.5), query * HEAD_DIM ** (-0.5)
        turned = small_key.T
        scores = nt(jnp.concatenate([key * halves[0], key * halves[1]], axis=0), query)
        changes = nt(jnp.concatenate([value * halves[0], value * halves[1]], axis=0), d_rows)
        queries, d_raws, lows = [], [], []
        for head in range(2):
            part = slice(head * PAD, (head + 1) * PAD)
            probs = jnp.exp2(real_keys(scores[part]) * SHARP - level[image, 2 * pair + head])
            d_probs = changes[part]
            delta = jnp.sum(probs * d_probs, 0, keepdims=True)
            d_raws.append((probs * (d_probs - delta)).astype(LOW))
            lows.append(probs.astype(LOW))
            queries.append(nn(turned[head * HEAD_DIM : (head + 1) * HEAD_DIM], d_raws[head]))
        both = jnp.concatenate(queries, axis=0).astype(LOW)
        d_qkv[rows, columns[0]] = both.T
        mine = lax.broadcasted_iota(jnp.int32, (PAD, WIDE), 1) < HEAD_DIM
        for third, parts, right in ((1, d_raws, small_query), (2, lows, d_rows)):
            sides = nn(jnp.concatenate(parts, axis=0), right)
            d_qkv[rows, columns[third]] = jnp.where(mine, sides[:PAD], sides[PAD:]).astype(LOW)

    def body(step):
        for at in range(3):
            one(step, at)

    over(2, body)


def bias_sums(d_qkv, vec_grad):
    def body(step, totals):
        rows = tile_of(step, STEP_ROWS)
        return (
            totals[0] + fold(d_qkv[rows, 0:D].astype(F32)),
            totals[1] + fold(d_qkv[rows, 2 * D : 3 * D].astype(F32)),
        )

    totals = lax.fori_loop(0, PADDED // STEP_ROWS, body, nothing(2), unroll=4)
    vec_grad[0:1, QUERY_BIAS : QUERY_BIAS + D] = column(totals[0])
    vec_grad[0:1, VALUE_BIAS : VALUE_BIAS + D] = column(totals[1])


def turn_into(turned, source, eye, first):
    for block in range(D // TILE):
        rows = slice(block * TILE, (block + 1) * TILE)
        columns = slice(first + block * TILE, first + (block + 1) * TILE)
        turned[rows, :] = nt(eye[...], source[:, columns]).astype(LOW)


def backward_kernel(drop, vec_rows, cotangent, full_ab, full_c, *rest):
    names = [name for name, _, _ in SAVED]
    saved = dict(zip(names, rest[: len(SAVED)]))
    rest = rest[len(SAVED) :]
    gradient, out, vec_out, square_out = rest[:4]
    held = dict(zip(names, rest[4 : 4 + len(SAVED)]))
    (
        weights, low, part, turned, eye, halves, vec_grad,
        made, near, side_a, side_b, last_a, last_b, line, final,
        vec_made, vec_mine, vec_near, vec_x, vec_y, vec_line, squares,
        load_sem, weight_sem, send, recv, own, credit, vec_send, vec_recv, sq_send, sq_recv,
    ) = rest[4 + len(SAVED) :]
    d_qkv, d_mixed = held["active"], held["normed_two"]
    count, half = 3 * LAYERS, ROWS // 2
    upper, lower = pl.ds(0, half), pl.ds(half, half)
    near_free, side_x, side_y, last_x, last_y = range(5)
    loads, arriving, sent = {}, {}, set()
    dp, fs, y, x, z, c = place()
    q_x, q_y = y * 2 + 1 - x, (1 - y) * 2 + x
    to_x, to_y, to_core = (q_x, fs), (q_y, fs), (dp, z * 2 + 1 - c)
    ahead = [lax.rem(z + k, 4) for k in (1, 2, 3)]
    to_line = [(dp, other * 2 + c) for other in ahead]
    to_cross = [(dp, other * 2 + 1 - c) for other in ahead]
    started, start = sender(send, recv)
    vec_started, vec_start = sender(vec_send, vec_recv)
    sq_started, sq_start = sender(sq_send, sq_recv)
    writes = {}
    course = Course()
    turns = [0]

    def turn(source, first=0):
        turns[0] += 1
        turn_into(turned.at[turns[0] % 2], source, eye, first)

    def give(which, device):
        pl.semaphore_signal(credit.at[which], inc=1, device_id=device, device_id_type=MESH_ID)

    def take_credit(*which):
        for at in which:
            pl.semaphore_wait(credit.at[at], 1)

    def leave(n, *which):
        for at in which:
            if (n, at) in started and (n, at) not in sent:
                started[n, at].wait_send()
                sent.add((n, at))

    def add(target, source):
        target[...] = target[...] + source[...]

    def fetch(layer, name):
        copy = pltpu.make_async_copy(
            saved[name].at[layer], held[name], load_sem.at[names.index(name)]
        )
        copy.start()
        loads[name] = copy

    def need(*which):
        for name in which:
            loads.pop(name).wait()

    def done(layer, *which):
        if layer > 0:
            for name in which:
                fetch(layer - 1, name)

    def fetch_weight(n):
        if n < count:
            layer, group = LAYERS - 1 - n // 3, 2 - n % 3
            arriving[n] = []
            for block in range(4):
                source = full_c.at[layer, block] if group == 2 else full_ab.at[layer, group, block]
                copy = pltpu.make_async_copy(
                    source, weights.at[n % 2, :, pl.ds(block * D, D)], weight_sem.at[n % 2, block]
                )
                copy.start()
                arriving[n].append(copy)

    def weight_of(n):
        for copy in arriving.pop(n):
            copy.wait()
        return weights.at[n % 2]

    def place_of(n, cc):
        other = lax.rem(cc + c, 2)
        return (1 - other) * (n % 3) + other * 3

    def begin(n):
        if n >= 3:
            course.require(n - 3, 4)
            leave(n - 3, *range(4, 13))
        if n >= 1:
            course.require(n - 1, 1)
            leave(n - 1, *range(4))
            take_credit(near_free)

    def push(n, j):
        if n % 3 == 0:
            start((n, j), (n, j), made.at[3, :, j], near.at[:, j], to_core)
        else:
            start((n, j), (n, j), made.at[3, j], near.at[j], to_core)

    def grad_columns(n, q, right, first):
        def body(step):
            columns = pl.ds(pl.multiple_of(first + step * TILE, TILE), TILE)
            values = nn(turned[turns[0] % 2], right[:, columns]).astype(LOW).reshape(4, 2, ROWS, TILE)
            for cc in range(2):
                made[place_of(n, cc), q, :, :, tile_of(step, TILE)] = values[:, cc]

        over(D // TILE, body, D // TILE)
        push(n, q)

    def grad_rows(n, zz):
        for first, cc, at, size in ((0, 0, 0, 256), (256, 0, 256, 128), (384, 1, 0, 128), (512, 1, 128, 256)):
            if first % TILE == 0:
                start_at = zz * D + first
                values = nn(turned[turns[0] % 2], held["active"][:, start_at : start_at + TILE])
                values = values.astype(LOW)
            cut = values[:, first % TILE : first % TILE + size].reshape(4, 2, ROWS, size)
            for side in range(2):
                lanes = slice(side * D // 2 + at, side * D // 2 + at + size)
                made[place_of(n, cc), :, zz, :, lanes] = cut[:, side]
        push(n, zz)

    def after_core(n):
        if n >= 2:
            course.require(n - 2, 2)
            take_credit(side_x, side_y)
        for j in range(4):
            started[n, j].wait_recv()

        def body(step):
            q, zz = lax.div(step, 4), lax.rem(step, 4)
            add(made.at[n % 3, q, zz], near.at[q, zz])

        over(16, body, 4)
        if n + 1 < count:
            give(near_free, to_core)
        mine = made.at[n % 3]
        for row in range(2):
            start((n, 4 + row), (n, 4 + row), mine.at[row * 2 + 1 - x, :, upper], side_a.at[n % 2, row], to_x)
            start((n, 6 + row), (n, 6 + row), mine.at[(1 - y) * 2 + row, :, lower], side_b.at[n % 2, row], to_y)

    def after_side(n):
        if n >= 2:
            course.require(n - 2, 3)
            take_credit(last_x, last_y)
        for at in range(4, 8):
            started[n, at].wait_recv()
        mine = made.at[n % 3]

        def body(zz):
            add(mine.at[q_y, zz, upper], side_a.at[n % 2, 1 - y, zz])
            add(mine.at[q_x, zz, lower], side_b.at[n % 2, 1 - x, zz])
            add(mine.at[dp, zz, upper], side_a.at[n % 2, y, zz])
            add(mine.at[dp, zz, lower], side_b.at[n % 2, x, zz])

        over(4, body, 2)
        if n + 2 < count:
            give(side_x, to_x)
            give(side_y, to_y)
        start((n, 8), (n, 8), mine.at[q_y, :, upper], last_a.at[n % 2], to_y)
        start((n, 9), (n, 9), mine.at[q_x, :, lower], last_b.at[n % 2], to_x)

    def after_last(n):
        started[n, 8].wait_recv()
        started[n, 9].wait_recv()
        mine = made.at[n % 3]

        def body(zz):
            add(mine.at[dp, zz, upper], last_a.at[n % 2, zz])
            add(mine.at[dp, zz, lower], last_b.at[n % 2, zz])

        over(4, body, 4)
        if n + 2 < count:
            give(last_x, to_x)
            give(last_y, to_y)
        for k in (1, 0, 2):
            start((n, 10 + k), (n, 10 + k), mine.at[dp, ahead[k]], line.at[n, k], to_line[k])

    def after_line(n):
        total = made[n % 3, dp, z].astype(F32)
        for k in range(3):
            started[n, 10 + k].wait_recv()
            total = total + line[n, k].astype(F32)
        final[n, dp] = total.astype(LOW)
        start((n, 13), (n, 13), final.at[n, dp], final.at[n, dp], to_x)
        start((n, 14), (n, 14), final.at[n, dp], final.at[n, dp], to_y)

    def after_sides(n):
        started[n, 13].wait_recv()
        piece = final.at[n, q_x, upper]
        start((n, 15), (n, 15), piece, piece, to_y)
        started[n, 14].wait_recv()
        piece = final.at[n, q_y, lower]
        start((n, 16), (n, 16), piece, piece, to_x)

    def finish(n):
        started[n, 15].wait_recv()
        started[n, 16].wait_recv()
        copy = pltpu.make_async_copy(final.at[n], out.at[LAYERS - 1 - n // 3, 2 - n % 3], own.at[n])
        copy.start()
        writes[n] = copy

        def body(step, total):
            values = final[n, lax.div(step, 6), tile_of(lax.rem(step, 6), 16)].astype(F32)
            values = values * values
            folded = values[0:8] + values[8:16]
            for at in range(6):
                total = total + folded[:, at * 128 : at * 128 + 128]
            return total

        square_out[...] += lax.fori_loop(0, 24, body, jnp.zeros((8, 128), F32), unroll=4)

    def ready(n):
        steps = (
            (after_core, "xy", 12.5),
            (after_side, "xy", 6.3),
            (after_last, "z", 12.5),
            (after_line, "xy", 3.2),
            (after_sides, "xy", 1.6),
            (finish, "none", 0.0),
        )
        course.add(n, [(functools.partial(step, n), link, cost) for step, link, cost in steps], 1.5)

    def vec_layer(layer):
        for at in range(72):
            shard, row = divmod(at, 9)
            vec_made[shard // 2, shard % 2, layer * 9 + row : layer * 9 + row + 1, :] = vec_grad[
                0:1, at * 128 : (at + 1) * 128
            ]

    def vec_core():
        vec_mine[...] = vec_made[:, c]
        vec_start(0, 0, vec_made.at[:, 1 - c], vec_near, to_core)

    def vec_sides():
        vec_started[0].wait_recv()
        vec_mine[...] = vec_mine[...] + vec_near[...]
        vec_start(1, 1, vec_mine, vec_x, to_x)

    def vec_second():
        vec_started[1].wait()
        vec_mine[...] = vec_mine[...] + vec_x[...]
        vec_start(2, 2, vec_mine, vec_y, to_y)

    def vec_third():
        vec_started[2].wait()
        vec_mine[...] = vec_mine[...] + vec_y[...]
        for k in range(3):
            vec_start(3 + k, 3 + k, vec_mine.at[ahead[k]], vec_line.at[z], to_line[k])
        vec_line[z] = vec_mine[z]

    def vec_last():
        for k in range(3):
            vec_started[3 + k].wait_recv()
        total = vec_line[0] + vec_line[1] + vec_line[2] + vec_line[3]
        vec_out[...] = total
        total = total * total
        square_out[...] += total[0:8] + total[8:16] + total[16:24]

    last = LAYERS - 1
    fetch(last, "active")
    fetch_weight(0)
    fetch(last, "slope")
    fetch(last, "normed_two")
    fetch_weight(1)
    for name in names:
        if name not in ("slope", "active", "normed_two"):
            fetch(last, name)
    square_out[...] = jnp.zeros((8, 128), F32)
    vec_made[...] = jnp.zeros((4, 2, 24, 128), F32)
    eye[...] = identity(TILE)
    head_lanes(halves)
    greet([to_x, to_y, to_core] + to_line + to_cross)
    for image in range(IMG_DEV):
        pad_image(gradient, cotangent, image)
    for layer in reversed(range(LAYERS)):
        row, base = vec_rows.at[pl.ds(layer, 1)], 3 * (LAYERS - 1 - layer)
        vec_grad[0:1, OUT_BIAS : OUT_BIAS + D] = scale_rows(gradient, low, drop, 2 * layer + 1)
        course.spend(2.0)
        need("active")
        begin(base)
        turn(low)
        for zz in range(4):
            grad_rows(base, zz)
            course.spend(2.5)
        ready(base)
        weight = weight_of(base)
        need("slope")
        for first in (0, 6):
            hidden_back(low, weight, held["slope"], vec_grad, first)
            course.spend(4.0)
        fetch_weight(base + 2)
        need("normed_two")
        turn(held["normed_two"])
        begin(base + 1)
        for q in range(4):
            grad_columns(base + 1, q, held["slope"], q * D)
            course.spend(2.0)
        ready(base + 1)
        weight = weight_of(base + 1)
        spread_back(held["slope"], weight, FF, part)
        fetch_weight(base + 3)
        course.spend(6.0)
        done(layer, "slope")
        need("unit_two", "scale_two")
        sums = norm_back(
            part, held["unit_two"], held["scale_two"], gradient, row[0:1, GAIN_TWO : GAIN_TWO + D],
            low, drop, 2 * layer,
        )
        done(layer, "unit_two", "scale_two")
        for at, total in zip((GAIN_TWO, SHIFT_TWO, PROJ_BIAS), sums):
            vec_grad[0:1, at : at + D] = total
        course.spend(3.0)
        weight = weight_of(base + 2)

        need("mixed")
        turn(held["mixed"])
        done(layer, "mixed")
        begin(base + 2)
        grad_columns(base + 2, 3, low, 0)
        course.spend(2.0)

        def mixed_body(step, weight=weight):
            tile = tile_of(step, TILE)
            d_mixed[:, tile] = nt(low[...], weight[tile, 3 * D : 4 * D]).astype(LOW)

        over(D // TILE, mixed_body, D // TILE)
        course.spend(1.5)
        need("qkv", "level")
        for image in range(IMG_DEV):
            attend_back(held["qkv"], held["level"], d_mixed, d_qkv, eye, halves, image)
            course.spend(4.5)
        done(layer, "qkv", "level", "normed_two")
        need("normed_one")
        turn(held["normed_one"])
        done(layer, "normed_one")
        for q in range(3):
            grad_columns(base + 2, q, d_qkv, q * D)
            course.spend(2.0)
        ready(base + 2)
        spread_back(d_qkv, weight, 3 * D, part)
        fetch_weight(base + 4)
        bias_sums(d_qkv, vec_grad)
        done(layer, "active")
        course.spend(6.0)
        need("unit_one", "scale_one")
        sums = norm_back(
            part, held["unit_one"], held["scale_one"], gradient, row[0:1, GAIN_ONE : GAIN_ONE + D]
        )
        done(layer, "unit_one", "scale_one")
        for at, total in zip((GAIN_ONE, SHIFT_ONE), sums):
            vec_grad[0:1, at : at + D] = total
        vec_layer(layer)
        course.spend(4.0)
    course.add(
        "vec",
        [(step, "none", 1.0) for step in (vec_core, vec_sides, vec_second, vec_third, vec_last)],
    )
    course.drain()
    squares[fs] = square_out[...]
    others = [(dp, lax.rem(fs + k, 8)) for k in range(1, 8)]
    for k in range(7):
        sq_start(k, k, squares.at[fs], squares.at[fs], others[k])
    for n in range(count):
        leave(n, *range(17))
        writes[n].wait()
    for k in (0, 3, 4, 5):
        vec_started[k].wait_send()
    for k in range(7):
        sq_started[k].wait_recv()
    total = squares[0]
    for k in range(1, 8):
        total = total + squares[k]
    square_out[...] = total
    for copy in sq_started.values():
        copy.wait_send()


def backward_call(drop, vec_rows, cotangent, full_ab, full_c, saved):
    dma = pltpu.SemaphoreType.DMA
    any_space = pl.BlockSpec(memory_space=pl.ANY)
    vmem = pl.BlockSpec(memory_space=pltpu.VMEM)
    count, half = 3 * LAYERS, ROWS // 2
    small = pltpu.VMEM((4, 24, 128), F32)
    return pl.pallas_call(
        backward_kernel,
        out_shape=[
            jax.ShapeDtypeStruct((PADDED, D), F32),
            jax.ShapeDtypeStruct((LAYERS, 3, 4, ROWS, D), LOW),
            jax.ShapeDtypeStruct((24, 128), F32),
            jax.ShapeDtypeStruct((8, 128), F32),
        ],
        in_specs=[pl.BlockSpec(memory_space=pltpu.SMEM), vmem, vmem] + [any_space] * (2 + len(SAVED)),
        out_specs=[vmem, any_space, vmem, vmem],
        scratch_shapes=[pltpu.VMEM(shape, kind) for _, shape, kind in SAVED]
        + [
            pltpu.VMEM((2, D, 4 * D), LOW),
            pltpu.VMEM((PADDED, D), LOW),
            pltpu.VMEM((PADDED, D), F32),
            pltpu.VMEM((2, D, PADDED), LOW),
            pltpu.VMEM((TILE, TILE), LOW),
            pltpu.VMEM((2, PAD, WIDE), LOW),
            pltpu.VMEM((1, WIDTH), F32),
            pltpu.VMEM((4, 4, 4, ROWS, D), LOW),
            pltpu.VMEM((4, 4, ROWS, D), LOW),
            pltpu.VMEM((2, 2, 4, half, D), LOW),
            pltpu.VMEM((2, 2, 4, half, D), LOW),
            pltpu.VMEM((2, 4, half, D), LOW),
            pltpu.VMEM((2, 4, half, D), LOW),
            pltpu.VMEM((count, 3, ROWS, D), LOW),
            pltpu.VMEM((count, 4, ROWS, D), LOW),
            pltpu.VMEM((4, 2, 24, 128), F32),
            small, small, small, small, small,
            pltpu.VMEM((8, 8, 128), F32),
            dma((len(SAVED),)),
            dma((2, 4)),
            dma((count, 17)),
            dma((count, 17)),
            dma((count,)),
            pltpu.SemaphoreType.REGULAR((5,)),
            dma((6,)),
            dma((6,)),
            dma((7,)),
            dma((7,)),
        ],
        compiler_params=pltpu.CompilerParams(
            collective_id=1, has_side_effects=True, vmem_limit_bytes=255 * MIB // 4
        ),
        name="backward_and_reduce",
    )(
        drop, vec_rows, cotangent,
        full_ab.reshape(LAYERS, 2, 4, D, D), full_c.reshape(LAYERS, 4, D, D),
        *[saved[name] for name, _, _ in SAVED],
    )


def update_kernel(vec_sum, squares, output, gradient, shares, *rest):
    masters, firsts, seconds = rest[:5], rest[5:10], rest[10:15]
    out_rows, grad_rows, norm = rest[15:18]
    results = [rest[18 + 3 * member : 21 + 3 * member] for member in range(5)]
    state, share, swapped, out_in, grad_in, out_cut, grad_cut, load_sem, share_sem, store_sem, row_sem = rest[33:]
    count = 3 * LAYERS

    def places(refs, i):
        layer, group = divmod(i, 3)
        if group == 0:
            found = [refs[0].at[layer, :, pl.ds(q * D, D)] for q in range(3)] + [refs[1].at[layer]]
        elif group == 1:
            found = [refs[2].at[layer, :, pl.ds(q * D, D)] for q in range(4)]
        else:
            found = [refs[3].at[layer, pl.ds(q * ROWS, ROWS)] for q in range(4)]
        return found

    loads, stores = {}, []
    for i in range(count):
        copy = pltpu.make_async_copy(shares.at[i // 3, i % 3], share.at[i], share_sem.at[i])
        copy.start()
        loads[i] = [copy]
        for kind, refs in enumerate((masters, firsts, seconds)):
            for q, source in enumerate(places(refs, i)):
                copy = pltpu.make_async_copy(source, state.at[kind, i, q], load_sem.at[kind, i, q])
                copy.start()
                loads[i].append(copy)

    rows_in = [(output, out_in), (gradient, grad_in)]
    rows_out = [(out_cut, out_rows), (grad_cut, grad_rows)]
    row_loads = []
    for at, (source, target) in enumerate(rows_in):
        copy = pltpu.make_async_copy(source, target, row_sem.at[at])
        copy.start()
        row_loads.append(copy)

    total = jnp.sqrt(jnp.sum(squares[...], keepdims=True))
    norm[...] = total
    factor = jnp.minimum(1.0, CLIP / (total + 1e-06))

    def step(weight, gradient_part, first, second, factor, member):
        return adamw_update(
            weight, gradient_part, first, second, factor, RATES[member], DECAYS[member]
        )

    for i in range(count):
        for copy in loads[i]:
            copy.wait()
        group = i % 3
        if group == 2:
            for q in range(4):
                for side in range(2):
                    rows = slice((2 * q + side) * ROWS, (2 * q + side + 1) * ROWS)
                    swapped[rows] = share[i, q, :, side * D // 2 : (side + 1) * D // 2]
            for block in range(3):
                columns = slice(block * 128, (block + 1) * 128)
                turned = nt(identity(128), swapped[:, columns]).astype(LOW)
                for at in range(block * 128, (block + 1) * 128, STEP_ROWS):
                    rows = slice(at % ROWS, at % ROWS + STEP_ROWS)
                    share[i, at // ROWS, rows] = turned[at % 128 : at % 128 + STEP_ROWS]
        for q in range(4):
            member = 1 if (group, q) == (0, 3) else (0, 2, 3)[group]

            def body(at, i=i, q=q, member=member):
                rows = tile_of(at, STEP_ROWS)
                clipped, moment, new = step(
                    state[0, i, q, rows],
                    share[i, q, rows].astype(F32),
                    state[1, i, q, rows],
                    state[2, i, q, rows],
                    factor,
                    member,
                )
                state[0, i, q, rows] = clipped
                state[1, i, q, rows] = moment
                state[2, i, q, rows] = new

            over(ROWS // STEP_ROWS, body, ROWS // STEP_ROWS)
            for kind in range(3):
                refs = [result[kind] for result in results]
                copy = pltpu.make_async_copy(
                    state.at[kind, i, q], places(refs, i)[q], store_sem.at[kind, i, q]
                )
                copy.start()
                stores.append(copy)
        if i == 2:
            for copy in row_loads:
                copy.wait()
            for image in range(IMG_DEV):
                rows, padded = slice(image * SEQ, (image + 1) * SEQ), slice(image * PAD, image * PAD + SEQ)
                out_cut[rows] = out_in[padded]
                grad_cut[rows] = grad_in[padded]
            for at, (source, target) in enumerate(rows_out):
                copy = pltpu.make_async_copy(source, target, row_sem.at[2 + at])
                copy.start()
                stores.append(copy)
    for layer in range(LAYERS):
        for part in range(9):
            columns = slice(part * 128, (part + 1) * 128)
            values = step(
                masters[4][layer : layer + 1, columns],
                vec_sum[layer * 9 + part : layer * 9 + part + 1],
                firsts[4][layer : layer + 1, columns],
                seconds[4][layer : layer + 1, columns],
                factor,
                4,
            )
            for kind in range(3):
                results[4][kind][layer : layer + 1, columns] = values[kind]
    for copy in stores:
        copy.wait()


def update_call(output, gradient, shares, vec_sum, squares, masters, firsts, seconds):
    dma = pltpu.SemaphoreType.DMA
    any_space = pl.BlockSpec(memory_space=pl.ANY)
    vmem = pl.BlockSpec(memory_space=pltpu.VMEM)
    count = 3 * LAYERS
    kinds = [any_space] * 4 + [vmem]
    outs = pl.pallas_call(
        update_kernel,
        out_shape=[
            jax.ShapeDtypeStruct((IMG_DEV * SEQ, D), LOW),
            jax.ShapeDtypeStruct((IMG_DEV * SEQ, D), F32),
            jax.ShapeDtypeStruct((1, 1), F32),
        ]
        + [jax.ShapeDtypeStruct(item.shape, F32) for item in masters for _ in range(3)],
        in_specs=[vmem] * 2 + [any_space] * 3 + kinds * 3,
        out_specs=[any_space] * 2 + [vmem] + [any_space] * 12 + [vmem] * 3,
        scratch_shapes=[
            pltpu.VMEM((3, count, 4, ROWS, D), F32),
            pltpu.VMEM((count, 4, ROWS, D), LOW),
            pltpu.VMEM((D, D // 2), LOW),
            pltpu.VMEM((PADDED, D), LOW),
            pltpu.VMEM((PADDED, D), F32),
            pltpu.VMEM((IMG_DEV * SEQ, D), LOW),
            pltpu.VMEM((IMG_DEV * SEQ, D), F32),
            dma((3, count, 4)),
            dma((count,)),
            dma((3, count, 4)),
            dma((4,)),
        ],
        compiler_params=pltpu.CompilerParams(vmem_limit_bytes=56 * MIB),
        name="update",
    )(vec_sum, squares, output, gradient, shares, *masters, *firsts, *seconds)
    return (outs[0], outs[1], outs[2].reshape(()), *outs[3:])


def exchange_plain(layer_grads):
    grads = [
        jnp.stack(
            [
                lax.psum(
                    lax.psum_scatter(parts[member], "fsdp", scatter_dimension=0, tiled=True), "dp"
                )
                for parts in layer_grads
            ]
        )
        for member in range(5)
    ]
    square = lax.psum(sum(jnp.sum(item * item) for item in grads), "fsdp")
    return grads, square


def gather_plain(*masters):
    return [
        tuple(
            lax.all_gather(item[at].astype(LOW), "fsdp", axis=0, tiled=True) for item in masters
        )
        for at in range(LAYERS)
    ]


def kernel_step(tokens, cotangent, keep_mask, masters, firsts, seconds):
    full, saved = forward_call(tokens, keep_mask, masters[4], masters[:4])
    full_ab, full_c, vec_rows, output = full
    gradient, shares, vec_sum, squares = backward_call(
        keep_mask, vec_rows, cotangent, full_ab, full_c, saved
    )
    return update_call(output, gradient, shares, vec_sum, squares, masters, firsts, seconds)


def plain_step(tokens, cotangent, keep_mask, masters, firsts, seconds):
    keep_float = keep_mask.astype(jnp.float32)
    vec_low = lax.all_gather(masters[4].astype(LOW), "fsdp", axis=1, tiled=True)
    matrices = gather_plain(*masters[:4])
    params = [matrices[at] + (vec_low[at],) for at in range(LAYERS)]
    stream = tokens.astype(jnp.float32)
    inputs = []
    for at in range(LAYERS):
        inputs.append(stream)
        stream, unused = block_forward(stream, params[at], keep_float[:, 2 * at : 2 * at + 2])
    output = stream.astype(LOW)
    grad_stream = cotangent.astype(jnp.float32)
    layer_grads = [None] * LAYERS
    for at in reversed(range(LAYERS)):
        grad_stream, layer_grads[at] = block_backward(
            inputs[at], params[at], keep_float[:, 2 * at : 2 * at + 2], grad_stream
        )
    grads, square = exchange_plain(layer_grads)
    grad_norm = jnp.sqrt(square)
    factor = jnp.minimum(1.0, CLIP / (grad_norm + 1e-06))
    updates = []
    for member in range(5):
        updates.extend(
            adamw_update(
                masters[member],
                grads[member],
                firsts[member],
                seconds[member],
                factor,
                RATES[member],
                DECAYS[member],
            )
        )
    return (output, grad_stream, grad_norm, *updates)


def on_device(kernels, tokens, cotangent, keep_mask, *state):
    masters, moments = state[:5], state[5:]
    step = kernel_step if kernels else plain_step
    return step(tokens, cotangent, keep_mask, masters, moments[0::2], moments[1::2])


def solution(mesh):
    rows = P(("dp", "fsdp"), None)
    matrix = P(None, "fsdp", None)
    vector = P(None, "fsdp")
    kernels = mesh.shape["dp"] == 4 and mesh.shape["fsdp"] == 8
    return jax.shard_map(
        functools.partial(on_device, kernels),
        mesh=mesh,
        in_specs=(rows,) * 3 + (matrix,) * 4 + (vector,) + (matrix,) * 8 + (vector,) * 2,
        out_specs=(rows, rows, P()) + (matrix,) * 12 + (vector,) * 3,
        check_vma=False,
    )
```
